32 devices in a mesh: pair: 4 (over z), row: 4 (over x, core), col: 2 (over y).
Axes of the slice: x: 2, y: 2, z: 4, core: 2. Of those that a mesh axis runs over, the one named last changes fastest.
Arguments:
- integrals: bfloat16 [3072, 4096], P(('pair', 'col')), may hold values from -0.15625 to 0.15625
- inverse_factor: bfloat16 [4096, 4096], P('row', ('pair', 'col')), may hold values from -4 to 4, as said below
- energies: float32 [3072], P('pair'), may hold values from 0.25 to 8
- frequency: float32 [1], replicated, may hold values from 0.5 to 2
Outputs:
- response: float32 [4096, 4096], P(('row', 'pair'), 'col')
The draws below stay inside these ranges and needn't reach their ends.
Inputs may be any that keep to these rules, and one draw needn't show every extreme that they name: `inverse_factor`: zero above the diagonal; the diagonal lies between 0.5 and 3.
All inputs are finite; a program needn't handle non-finite values.
Results may differ from the reference program's by a relative error of at most 0.0025.
Values may be sent and summed in bfloat16 or wider, within the bound.
No kernel may reach another device: no remote copies, remote signals or barrier semaphores. Data moves between devices by JAX's collectives and lax.ppermute only.
A program may use at most 64 MiB of HBM per device.

```python
import math
import jax
import jax.numpy as jnp
from jax import lax

NAUX = 4096
PAIRS = 3072


def draw_inverse_factor(key, part):
    key_lower, key_diag = jax.random.split(jax.random.fold_in(key, 7))
    row_index = lax.broadcasted_iota(jnp.int32, (NAUX, NAUX), 0)
    col_index = lax.broadcasted_iota(jnp.int32, (NAUX, NAUX), 1)
    lower_part = jnp.clip(jax.random.normal(key_lower, (NAUX, NAUX), jnp.float32), -6.0, 6.0)
    diagonal_part = jax.random.uniform(key_diag, (NAUX, NAUX), jnp.float32, 1.0, 2.0)
    row_scale = 0.5 * lax.rsqrt(row_index.astype(jnp.float32) + 1.0)
    values = jnp.where(row_index == col_index, diagonal_part, jnp.where(col_index < row_index, lower_part * row_scale, 0.0))
    return values.astype(jnp.bfloat16)


def with_spikes(drawn, own_key, source, target, shards_of, factor):
    owner, partner = [(jnp.arange(drawn.shape[axis_at]) // (drawn.shape[axis_at] // shards_of)).reshape([-1 if axis == axis_at else 1 for axis in range(drawn.ndim)]) for axis_at in (source, target)]
    chosen = jax.random.permutation(own_key, shards_of)[partner]
    strong = (owner == chosen) | (owner == (partner + shards_of // 2) % shards_of)
    return jnp.where(strong, factor * drawn, drawn)


def levels(own_key, shape, pieces, least, top_value):
    level = 1.0
    for dim, shards_of in pieces:
        steps = jax.random.uniform(jax.random.fold_in(jax.random.fold_in(own_key, 6), dim), (shards_of,), jnp.float32, least / len(pieces), top_value / len(pieces))
        level = level * jnp.repeat(jnp.exp(steps), shape[dim] // shards_of).reshape((-1,) + (1,) * (len(shape) - 1 - dim))
    return level


def heavy_noise(stream_key, dims, scale, reach, pieces, heavy, kind=jnp.bfloat16):
    array = scale * jax.random.normal(stream_key, dims, jnp.float32)
    if pieces:
        array = array * levels(stream_key, dims, pieces, -0.22, 0.18)
    return jnp.clip(with_spikes(array, jax.random.fold_in(stream_key, 3), *heavy), -reach, reach).astype(kind)


def setup_inputs(seed: int = 0) -> dict:
    keys = jax.random.split(jax.random.key(seed), 5)
    return {
        "integrals": heavy_noise(keys[0], (PAIRS, NAUX), (PAIRS ** -0.5), 0.15625, ((0, 8),), (0, 1, 8, 2.0)),
        "inverse_factor": draw_inverse_factor(jax.random.fold_in(keys[4], 71), 0),
        "energies": jnp.clip(jnp.exp(math.log(8.0) - 3.465736 * jax.random.uniform(keys[2], (PAIRS,), jnp.float32) ** levels(keys[2], (PAIRS,), ((0, 4),), -0.2, 0.2)), 0.25, 8.0),
        "frequency": jnp.clip(jnp.exp(jax.random.uniform(keys[3], (1,), jnp.float32, math.log(0.5), math.log(2.0))), 0.5, 2.0),
    }


def reference(integrals, inverse_factor, energies, frequency):
    transformed = lax.dot_general(integrals, inverse_factor, (((1,), (1,)), ((), ())), preferred_element_type=jnp.float32).astype(jnp.bfloat16)
    factor = 2.0 * energies / (energies * energies + frequency[0] * frequency[0])
    scaled = (factor[:, None] * transformed.astype(jnp.float32)).astype(jnp.bfloat16)
    return lax.dot_general(scaled, transformed, (((0,), (0,)), ((), ())), preferred_element_type=jnp.float32)
```

```python
import jax
import jax.numpy as jnp
from jax import lax
from jax.sharding import PartitionSpec as P

AXES = ("pair", "row", "col")
BF16 = jnp.bfloat16
F32 = jnp.float32


def rows_by_rows(a, b):
    return lax.dot_general(a, b, (((1,), (1,)), ((), ())), preferred_element_type=F32)


def columns_by_columns(a, b):
    return lax.dot_general(a, b, (((0,), (0,)), ((), ())), preferred_element_type=F32)


def scale_of(energies, frequency):
    return 2.0 * energies / (energies * energies + frequency[0] * frequency[0])


def any_mesh(integrals, inverse_factor, energies, frequency):
    n_col = lax.axis_size("col")
    q_cols = integrals.shape[1] // n_col
    local_rows = rows_by_rows(
        integrals, lax.all_gather(inverse_factor, ("pair", "col"), axis=1, tiled=True)
    )
    group_b = lax.all_gather(local_rows.astype(BF16), "col", axis=0, tiled=True)
    portion = lax.all_gather(group_b, "row", axis=1, tiled=True)
    col_b = lax.dynamic_slice_in_dim(
        portion, lax.axis_index("col") * q_cols, q_cols, axis=1
    )
    factor = scale_of(energies, frequency)
    scaled = (factor[:, None] * group_b.astype(F32)).astype(BF16)
    return lax.psum_scatter(
        columns_by_columns(scaled, col_b), "pair", scatter_dimension=0, tiled=True
    )


def route(target):
    def index(z, x, k, y):
        return ((z * 2 + x) * 2 + k) * 2 + y

    pairs = []
    for z in range(4):
        for x in range(2):
            for k in range(2):
                for y in range(2):
                    to = target(z, x, k, y)
                    if to is not None:
                        pairs.append((index(z, x, k, y), index(*to)))
    return pairs


def send(value, pairs):
    return lax.ppermute(value, AXES, pairs)


OVER_X = route(lambda z, x, k, y: (z, 1 - x, k, y))
OVER_Y = route(lambda z, x, k, y: (z, x, k, 1 - y))
OVER_XY = route(lambda z, x, k, y: (z, 1 - x, k, 1 - y))
OVER_CORE = route(lambda z, x, k, y: (z, x, 1 - k, y))


def along_z(step, allowed):
    def target(z, x, k, y):
        if 0 <= z + step < 4 and allowed(z, k):
            return (z + step, x, k, y)
        return None

    return route(target)


def four_planes(integrals, inverse_factor, energies, frequency):
    z = lax.axis_index("pair")
    row = lax.axis_index("row")
    x, k = row // 2, row % 2
    y = lax.axis_index("col")
    chip = 2 * x + y
    mine = integrals
    n_rows, width = inverse_factor.shape
    piece = n_rows // 4

    half = mine.shape[0] // 2
    from_y = send(lax.dynamic_slice_in_dim(mine, k * half, half, 0), OVER_Y)
    from_core = send(from_y, OVER_CORE)
    theirs = jnp.concatenate(
        [jnp.where(k == 0, from_y, from_core), jnp.where(k == 0, from_core, from_y)], 0
    )

    def quarter(c):
        return lax.dynamic_slice_in_dim(inverse_factor, c * piece, piece, 0)

    own = quarter(chip)
    got_y = send(quarter(chip ^ 1), OVER_Y)
    got_x = send(quarter(chip ^ 2), OVER_X)
    got_xy = send(quarter(chip ^ 3), OVER_XY)

    def by_y(a, b):
        return jnp.concatenate([jnp.where(y == 0, a, b), jnp.where(y == 0, b, a)], 1)

    same, other = by_y(own, got_y), by_y(got_x, got_xy)
    parts = [jnp.where(x == 0, same, other), jnp.where(x == 0, other, same)]

    def term(values, plane):
        at = jnp.clip(plane, 0, 3) * 2 * width
        return [
            rows_by_rows(lax.dynamic_slice_in_dim(a, at, 2 * width, 1), values)
            for a in (mine, theirs)
        ]

    totals = [term(parts[p], z) for p in range(2)]
    moving = [[parts[p], parts[p]] for p in range(2)]
    for step in range(1, 4):
        for d in (0, 1):
            sign = 1 - 2 * d
            for p in range(2):

                def allowed(at, core):
                    source = at - sign * (step - 1)
                    return 0 <= source < 4 and source <= 2 * p + core

                pairs = along_z(sign, allowed)
                if not pairs:
                    continue
                moving[p][d] = send(moving[p][d], pairs)
                more = term(moving[p][d], z - sign * step)
                totals[p] = [t + m for t, m in zip(totals[p], more)]

    def ordered(a, b):
        a, b = a.astype(BF16), b.astype(BF16)
        return jnp.concatenate([jnp.where(y == 0, a, b), jnp.where(y == 0, b, a)], 0)

    low, high = ordered(*totals[0]), ordered(*totals[1])

    low_y, high_y = send(low, OVER_Y), send(high, OVER_Y)
    low_x, high_x = send(low, OVER_X), send(high, OVER_X)
    low_xy, high_xy = send(low_y, OVER_X), send(high_x, OVER_Y)
    lows = [low, low_y, low_x, low_xy]
    highs = [high, high_y, high_x, high_xy]
    row_parts = [jnp.where(x == 0, a, b) for a, b in zip(lows, highs)]
    col_parts = [jnp.where(y == 0, a, b) for a, b in zip(lows, highs)]
    columns = jnp.concatenate(col_parts, 1)
    core_columns = send(columns, OVER_CORE)

    factor = scale_of(energies, frequency)
    rows = jnp.concatenate(row_parts, 1)
    scaled = (factor[:, None] * rows.astype(F32)).astype(BF16)

    def block(plane, cols):
        at = (plane ^ chip) * piece
        return columns_by_columns(lax.dynamic_slice_in_dim(scaled, at, piece, 1), cols)

    def to_right(hop):
        return along_z(1, lambda at, core: at < hop)

    def to_left(hop):
        return along_z(-1, lambda at, core: at > 3 - hop)

    def summed(cols):
        far = block(z ^ 3, cols)
        right = send(far.astype(BF16), to_right(1))
        left = send(far.astype(BF16), to_left(1))
        next_far = block(z ^ 2, cols)
        right = send((next_far + right.astype(F32)).astype(BF16), to_right(2))
        left = send((next_far + left.astype(F32)).astype(BF16), to_left(2))
        near = block(z ^ 1, cols)
        right = (jnp.where(z == 1, far, near) + right.astype(F32)).astype(BF16)
        left = (jnp.where(z == 2, far, near) + left.astype(F32)).astype(BF16)
        right, left = send(right, to_right(3)), send(left, to_left(3))
        return block(z, cols) + right.astype(F32) + left.astype(F32)

    sums = jnp.stack([summed(columns), summed(core_columns)])
    out = [
        lax.dynamic_slice(
            sums, (c ^ k, 0, (q ^ chip) * piece), (1, piece, piece)
        ).reshape(piece, piece)
        for c in range(2)
        for q in range(4)
    ]
    return jnp.concatenate(out, 1)


def solution(mesh):
    planes = tuple(mesh.shape[a] for a in AXES) == (4, 4, 2)
    return jax.shard_map(
        four_planes if planes else any_mesh,
        mesh=mesh,
        in_specs=(P(("pair", "col"), None), P("row", ("pair", "col")), P("pair"), P()),
        out_specs=P(("row", "pair"), "col"),
        check_vma=False,
    )
```

```python
import jax
import jax.numpy as jnp
from jax import lax
from jax.sharding import PartitionSpec as P

AXES = ("pair", "row", "col")
BF16 = jnp.bfloat16
F32 = jnp.float32


def rows_by_rows(a, b):
    return lax.dot_general(a, b, (((1,), (1,)), ((), ())), preferred_element_type=F32)


def columns_by_columns(a, b):
    return lax.dot_general(a, b, (((0,), (0,)), ((), ())), preferred_element_type=F32)


def scale_of(energies, frequency):
    return 2.0 * energies / (energies * energies + frequency[0] * frequency[0])


def any_mesh(integrals, inverse_factor, energies, frequency):
    n_col = lax.axis_size("col")
    q_cols = integrals.shape[1] // n_col
    local_rows = rows_by_rows(
        integrals, lax.all_gather(inverse_factor, ("pair", "col"), axis=1, tiled=True)
    )
    group_b = lax.all_gather(local_rows.astype(BF16), "col", axis=0, tiled=True)
    portion = lax.all_gather(group_b, "row", axis=1, tiled=True)
    col_b = lax.dynamic_slice_in_dim(
        portion, lax.axis_index("col") * q_cols, q_cols, axis=1
    )
    factor = scale_of(energies, frequency)
    scaled = (factor[:, None] * group_b.astype(F32)).astype(BF16)
    return lax.psum_scatter(
        columns_by_columns(scaled, col_b), "pair", scatter_dimension=0, tiled=True
    )


def route(target):
    def index(z, x, k, y):
        return ((z * 2 + x) * 2 + k) * 2 + y

    pairs = []
    for z in range(4):
        for x in range(2):
            for k in range(2):
                for y in range(2):
                    to = target(z, x, k, y)
                    if to is not None:
                        pairs.append((index(z, x, k, y), index(*to)))
    return pairs


def send(value, pairs):
    return lax.ppermute(value, AXES, pairs)


OVER_X = route(lambda z, x, k, y: (z, 1 - x, k, y))
OVER_Y = route(lambda z, x, k, y: (z, x, k, 1 - y))
OVER_XY = route(lambda z, x, k, y: (z, 1 - x, k, 1 - y))
OVER_CORE = route(lambda z, x, k, y: (z, x, 1 - k, y))


def along_z(step, allowed):
    def target(z, x, k, y):
        if 0 <= z + step < 4 and allowed(z, k):
            return (z + step, x, k, y)
        return None

    return route(target)


def four_planes(integrals, inverse_factor, energies, frequency):
    z = lax.axis_index("pair")
    row = lax.axis_index("row")
    x, k = row // 2, row % 2
    y = lax.axis_index("col")
    chip = 2 * x + y
    n_rows, width = inverse_factor.shape
    piece = n_rows // 4

    quarters = lax.optimization_barrier(
        [
            lax.dynamic_slice_in_dim(inverse_factor, (chip ^ c) * piece, piece, 0)
            for c in range(4)
        ]
    )
    own = quarters[0]
    got_y = send(quarters[1], OVER_Y)
    got_x = send(quarters[2], OVER_X)
    got_xy = send(quarters[3], OVER_XY)

    half = integrals.shape[0] // 2
    from_y = send(lax.dynamic_slice_in_dim(integrals, k * half, half, 0), OVER_Y)
    from_core = send(from_y, OVER_CORE)
    theirs = jnp.concatenate(
        [jnp.where(k == 0, from_y, from_core), jnp.where(k == 0, from_core, from_y)], 0
    )
    factors = scale_of(lax.all_gather(energies, "pair"), frequency)

    def by_y(a, b, axis):
        return jnp.concatenate([jnp.where(y == 0, a, b), jnp.where(y == 0, b, a)], axis)

    same, other = by_y(own, got_y, 1), by_y(got_x, got_xy, 1)
    parts = [jnp.where(x == 0, same, other), jnp.where(x == 0, other, same)]

    def term(values, plane):
        at = jnp.clip(plane, 0, 3) * 2 * width
        return [
            rows_by_rows(values, lax.dynamic_slice_in_dim(a, at, 2 * width, 1))
            for a in (integrals, theirs)
        ]

    totals = [term(parts[p], z) for p in range(2)]
    moving = [[parts[p], parts[p]] for p in range(2)]
    for step in range(1, 4):
        for d in (0, 1):
            sign = 1 - 2 * d
            for p in range(2):

                def allowed(at, core):
                    source = at - sign * (step - 1)
                    return 0 <= source < 4 and source <= 2 * p + core

                pairs = along_z(sign, allowed)
                if not pairs:
                    continue
                moving[p][d] = send(moving[p][d], pairs)
                more = term(moving[p][d], z - sign * step)
                totals[p] = [t + m for t, m in zip(totals[p], more)]

    low, high = [
        by_y(totals[p][0].astype(BF16), totals[p][1].astype(BF16), 1) for p in range(2)
    ]

    keep, give = jnp.where(y == 0, low, high), jnp.where(y == 0, high, low)
    plane = by_y(keep, send(give, OVER_Y), 0)

    def hops(step):
        last = plane
        for hop in range(3):
            here = (lambda at, core: at >= hop) if step == 1 else (lambda at, core: at <= 3 - hop)
            last = send(last, along_z(step, here))
            yield last

    right, left = list(hops(1)), list(hops(-1))
    planes = [
        plane,
        jnp.where(z % 2 == 1, right[0], left[0]),
        jnp.where(z < 2, left[1], right[1]),
        jnp.where(
            z < 2,
            jnp.where(z == 0, left[2], left[0]),
            jnp.where(z == 2, right[0], right[2]),
        ),
    ]

    def to_rows(zz, xx, kk, yy):
        at = zz // 2
        if xx != at:
            return None
        return (zz, at, kk, 1 - at) if yy == at else (zz, 1 - at, kk, at)

    blocks = [0.0] * 4
    for i, mine in enumerate(planes):
        beside = send(mine, OVER_X)
        core_mine, core_beside = send(mine, OVER_CORE), send(beside, OVER_CORE)

        def chunk(a):
            return lax.dynamic_slice_in_dim(a, (z % 2) * piece, piece, 0)

        there = send(chunk(mine), route(to_rows))
        rows = jnp.where(
            x != y, there, jnp.where(x == z // 2, chunk(mine), chunk(beside))
        )
        factor = lax.dynamic_slice_in_dim(factors, z ^ i, 1, 0)
        scaled = (factor * rows.astype(F32)).astype(BF16)
        blocks = [
            b + rows_by_rows(scaled, columns)
            for b, columns in zip(blocks, (mine, beside, core_mine, core_beside))
        ]

    def at(core, side):
        by_x = [jnp.where(x == side, blocks[2 * c], blocks[2 * c + 1]) for c in (0, 1)]
        return jnp.where(k == core, by_x[0], by_x[1])

    return jnp.concatenate([at(c, s) for c in (0, 1) for s in (0, 1)], 1)


def solution(mesh):
    planes = tuple(mesh.shape[a] for a in AXES) == (4, 4, 2)
    return jax.shard_map(
        four_planes if planes else any_mesh,
        mesh=mesh,
        in_specs=(P(("pair", "col"), None), P("row", ("pair", "col")), P("pair"), P()),
        out_specs=P(("row", "pair"), "col"),
        check_vma=False,
    )
```

```python
import jax
import jax.numpy as jnp
from jax import lax
from jax.sharding import PartitionSpec as P

AXES = ("pair", "row", "col")
BF16 = jnp.bfloat16
F32 = jnp.float32


def rows_by_rows(a, b):
    return lax.dot_general(a, b, (((1,), (1,)), ((), ())), preferred_element_type=F32)


def columns_by_columns(a, b):
    return lax.dot_general(a, b, (((0,), (0,)), ((), ())), preferred_element_type=F32)


def scale_of(energies, frequency):
    return 2.0 * energies / (energies * energies + frequency[0] * frequency[0])


def any_mesh(integrals, inverse_factor, energies, frequency):
    n_col = lax.axis_size("col")
    q_cols = integrals.shape[1] // n_col
    local_rows = rows_by_rows(
        integrals, lax.all_gather(inverse_factor, ("pair", "col"), axis=1, tiled=True)
    )
    group_b = lax.all_gather(local_rows.astype(BF16), "col", axis=0, tiled=True)
    portion = lax.all_gather(group_b, "row", axis=1, tiled=True)
    col_b = lax.dynamic_slice_in_dim(
        portion, lax.axis_index("col") * q_cols, q_cols, axis=1
    )
    factor = scale_of(energies, frequency)
    scaled = (factor[:, None] * group_b.astype(F32)).astype(BF16)
    return lax.psum_scatter(
        columns_by_columns(scaled, col_b), "pair", scatter_dimension=0, tiled=True
    )


def route(target):
    def index(z, x, k, y):
        return ((z * 2 + x) * 2 + k) * 2 + y

    pairs = []
    for z in range(4):
        for x in range(2):
            for k in range(2):
                for y in range(2):
                    to = target(z, x, k, y)
                    if to is not None:
                        pairs.append((index(z, x, k, y), index(*to)))
    return pairs


def send(value, pairs):
    return lax.ppermute(value, AXES, pairs)


OVER_X = route(lambda z, x, k, y: (z, 1 - x, k, y))
OVER_Y = route(lambda z, x, k, y: (z, x, k, 1 - y))
OVER_XY = route(lambda z, x, k, y: (z, 1 - x, k, 1 - y))
OVER_CORE = route(lambda z, x, k, y: (z, x, 1 - k, y))


def along_z(step, allowed):
    def target(z, x, k, y):
        if 0 <= z + step < 4 and allowed(z, k):
            return (z + step, x, k, y)
        return None

    return route(target)


def four_planes(integrals, inverse_factor, energies, frequency):
    z = lax.axis_index("pair")
    row = lax.axis_index("row")
    x, k = row // 2, row % 2
    y = lax.axis_index("col")
    chip = 2 * x + y
    mine = integrals
    n_rows, width = inverse_factor.shape
    piece = n_rows // 4

    own, *others = lax.optimization_barrier(
        [
            lax.dynamic_slice_in_dim(inverse_factor, (chip ^ c) * piece, piece, 0)
            for c in range(4)
        ]
    )
    got_y, got_x, got_xy = (
        send(q, r) for q, r in zip(others, (OVER_Y, OVER_X, OVER_XY))
    )

    half = mine.shape[0] // 2
    give = lax.dynamic_slice_in_dim(mine, k * half, half, 0)
    from_y = send(lax.optimization_barrier((give, got_y, got_x, got_xy))[0], OVER_Y)
    from_core = send(from_y, OVER_CORE)
    theirs = jnp.concatenate(
        [jnp.where(k == 0, from_y, from_core), jnp.where(k == 0, from_core, from_y)], 0
    )

    def by_y(a, b):
        return jnp.concatenate([jnp.where(y == 0, a, b), jnp.where(y == 0, b, a)], 1)

    same, other = by_y(own, got_y), by_y(got_x, got_xy)
    parts = [jnp.where(x == 0, same, other), jnp.where(x == 0, other, same)]

    def term(values, plane):
        at = jnp.clip(plane, 0, 3) * 2 * width
        return [
            rows_by_rows(lax.dynamic_slice_in_dim(a, at, 2 * width, 1), values)
            for a in (mine, theirs)
        ]

    totals = [term(parts[p], z) for p in range(2)]
    moving = [[parts[p], parts[p]] for p in range(2)]
    for step in range(1, 4):
        for d in (0, 1):
            sign = 1 - 2 * d
            for p in range(2):

                def allowed(at, core):
                    source = at - sign * (step - 1)
                    return 0 <= source < 4 and source <= 2 * p + core

                pairs = along_z(sign, allowed)
                if not pairs:
                    continue
                moving[p][d] = send(moving[p][d], pairs)
                more = term(moving[p][d], z - sign * step)
                totals[p] = [t + m for t, m in zip(totals[p], more)]

    def ordered(a, b):
        a, b = a.astype(BF16), b.astype(BF16)
        return jnp.concatenate([jnp.where(y == 0, a, b), jnp.where(y == 0, b, a)], 0)

    low, high = ordered(*totals[0]), ordered(*totals[1])

    low_y, high_y = send(low, OVER_Y), send(high, OVER_Y)
    low_x, high_x = send(low, OVER_X), send(high, OVER_X)
    low_xy, high_xy = send(low_y, OVER_X), send(high_x, OVER_Y)
    lows = [low, low_y, low_x, low_xy]
    highs = [high, high_y, high_x, high_xy]
    row_parts = [jnp.where(x == 0, a, b) for a, b in zip(lows, highs)]
    col_parts = [jnp.where(y == 0, a, b) for a, b in zip(lows, highs)]
    columns = jnp.concatenate(col_parts, 1)
    core_columns = send(columns, OVER_CORE)

    factor = scale_of(energies, frequency)
    rows = jnp.concatenate(row_parts, 1)
    scaled = (factor[:, None] * rows.astype(F32)).astype(BF16)

    def block(plane, cols):
        at = (plane ^ chip) * piece
        return columns_by_columns(lax.dynamic_slice_in_dim(scaled, at, piece, 1), cols)

    def to_right(hop):
        return along_z(1, lambda at, core: at < hop)

    def to_left(hop):
        return along_z(-1, lambda at, core: at > 3 - hop)

    def summed(cols):
        far = block(z ^ 3, cols)
        right = send(far.astype(BF16), to_right(1))
        left = send(far.astype(BF16), to_left(1))
        next_far = block(z ^ 2, cols)
        right = send((next_far + right.astype(F32)).astype(BF16), to_right(2))
        left = send((next_far + left.astype(F32)).astype(BF16), to_left(2))
        near = block(z ^ 1, cols)
        right = (jnp.where(z == 1, far, near) + right.astype(F32)).astype(BF16)
        left = (jnp.where(z == 2, far, near) + left.astype(F32)).astype(BF16)
        right, left = send(right, to_right(3)), send(left, to_left(3))
        return block(z, cols) + right.astype(F32) + left.astype(F32)

    sums = jnp.stack([summed(columns), summed(core_columns)])
    out = [
        lax.dynamic_slice(
            sums, (c ^ k, 0, (q ^ chip) * piece), (1, piece, piece)
        ).reshape(piece, piece)
        for c in range(2)
        for q in range(4)
    ]
    return jnp.concatenate(out, 1)


def solution(mesh):
    planes = tuple(mesh.shape[a] for a in AXES) == (4, 4, 2)
    return jax.shard_map(
        four_planes if planes else any_mesh,
        mesh=mesh,
        in_specs=(P(("pair", "col"), None), P("row", ("pair", "col")), P("pair"), P()),
        out_specs=P(("row", "pair"), "col"),
        check_vma=False,
    )
```

```python
import jax
import jax.numpy as jnp
from jax import lax
from jax.sharding import PartitionSpec as P

AXES = ("pair", "row", "col")
BF16 = jnp.bfloat16
F32 = jnp.float32


def rows_by_rows(a, b):
    return lax.dot_general(a, b, (((1,), (1,)), ((), ())), preferred_element_type=F32)


def columns_by_columns(a, b):
    return lax.dot_general(a, b, (((0,), (0,)), ((), ())), preferred_element_type=F32)


def scale_of(energies, frequency):
    return 2.0 * energies / (energies * energies + frequency[0] * frequency[0])


def any_mesh(integrals, inverse_factor, energies, frequency):
    n_col = lax.axis_size("col")
    q_cols = integrals.shape[1] // n_col
    local_rows = rows_by_rows(
        integrals, lax.all_gather(inverse_factor, ("pair", "col"), axis=1, tiled=True)
    )
    group_b = lax.all_gather(local_rows.astype(BF16), "col", axis=0, tiled=True)
    portion = lax.all_gather(group_b, "row", axis=1, tiled=True)
    col_b = lax.dynamic_slice_in_dim(
        portion, lax.axis_index("col") * q_cols, q_cols, axis=1
    )
    factor = scale_of(energies, frequency)
    scaled = (factor[:, None] * group_b.astype(F32)).astype(BF16)
    return lax.psum_scatter(
        columns_by_columns(scaled, col_b), "pair", scatter_dimension=0, tiled=True
    )


def route(target):
    def index(z, x, k, y):
        return ((z * 2 + x) * 2 + k) * 2 + y

    pairs = []
    for z in range(4):
        for x in range(2):
            for k in range(2):
                for y in range(2):
                    to = target(z, x, k, y)
                    if to is not None:
                        pairs.append((index(z, x, k, y), index(*to)))
    return pairs


def send(value, pairs):
    return lax.ppermute(value, AXES, pairs)


OVER_X = route(lambda z, x, k, y: (z, 1 - x, k, y))
OVER_Y = route(lambda z, x, k, y: (z, x, k, 1 - y))
OVER_XY = route(lambda z, x, k, y: (z, 1 - x, k, 1 - y))
OVER_CORE = route(lambda z, x, k, y: (z, x, 1 - k, y))


def along_z(step, allowed):
    def target(z, x, k, y):
        if 0 <= z + step < 4 and allowed(z, k):
            return (z + step, x, k, y)
        return None

    return route(target)


def row_block(stream, x, k):
    return 2 * (x if stream == 0 else 1 - x) + k


def z_hops(part, sign, step):
    def target(z, x, k, y):
        source, p = z - sign * (step - 1), part
        if 0 <= z + sign < 4 and 0 <= source < 4 and source <= 2 * p + k:
            return (z + sign, x, k, y)
        return None

    return route(target)


def four_planes(integrals, inverse_factor, energies, frequency):
    z = lax.axis_index("pair")
    row = lax.axis_index("row")
    x, k = row // 2, row % 2
    y = lax.axis_index("col")
    chip = 2 * x + y
    n_rows, width = inverse_factor.shape
    piece = n_rows // 4

    def ordered(flag, a, b, axis):
        return jnp.concatenate(
            [jnp.where(flag == 0, a, b), jnp.where(flag == 0, b, a)], axis
        )

    own, *others = lax.optimization_barrier(
        [
            lax.dynamic_slice_in_dim(inverse_factor, (chip ^ c) * piece, piece, 0)
            for c in range(4)
        ]
    )
    got = [send(q, r) for q, r in zip(others, (OVER_Y, OVER_X, OVER_XY))]
    same, other = ordered(y, own, got[0], 1), ordered(y, got[1], got[2], 1)
    parts = [jnp.where(x == 0, same, other), jnp.where(x == 0, other, same)]
    half = integrals.shape[0] // 2
    give = lax.dynamic_slice_in_dim(integrals, k * half, half, 0)
    from_y = send(give, OVER_Y)
    from_core = send(from_y, OVER_CORE)
    theirs = ordered(k, from_y, from_core, 0)

    def term(values, away):
        at = jnp.clip(z + away, 0, 3) * 2 * width
        return [
            rows_by_rows(lax.dynamic_slice_in_dim(a, at, 2 * width, 1), values)
            for a in (integrals, theirs)
        ]

    came = [[(parts[p], 0)] for p in range(2)]
    moving = [[parts[p], parts[p]] for p in range(2)]
    for step in (1, 2, 3):
        for d in (0, 1):
            for p in (0, 1):
                sign = 1 - 2 * d
                pairs = z_hops(p, sign, step)
                if pairs:
                    moving[p][d] = send(moving[p][d], pairs)
                    came[p].append((moving[p][d], -sign * step))
    totals = []
    for p in range(2):
        total = term(*came[p][0])
        for value, away in came[p][1:]:
            total = [t + m for t, m in zip(total, term(value, away))]
        totals.append(total)
    straight, across = [
        ordered(y, t[0].astype(BF16), t[1].astype(BF16), 0) for t in totals
    ]

    straight_y, across_y = send(straight, OVER_Y), send(across, OVER_Y)
    straight_x, across_x = send(straight, OVER_X), send(across, OVER_X)
    straight_xy, across_xy = send(straight_y, OVER_X), send(across_x, OVER_Y)
    lows = [straight, straight_y, straight_x, straight_xy]
    highs = [across, across_y, across_x, across_xy]
    rows = jnp.concatenate([jnp.where(x == 0, a, b) for a, b in zip(lows, highs)], 1)
    columns = jnp.concatenate(
        [jnp.where(y == 0, a, b) for a, b in zip(lows, highs)], 1
    )
    core_columns = send(columns, OVER_CORE)
    factor = scale_of(energies, frequency)
    scaled = (factor[:, None] * rows.astype(F32)).astype(BF16)

    def block(plane, cols):
        at = (plane ^ chip) * piece
        return columns_by_columns(lax.dynamic_slice_in_dim(scaled, at, piece, 1), cols)

    def to_right(hop):
        return along_z(1, lambda at, core: at < hop)

    def to_left(hop):
        return along_z(-1, lambda at, core: at > 3 - hop)

    def summed(cols):
        far = block(z ^ 3, cols)
        right = send(far.astype(BF16), to_right(1))
        left = send(far.astype(BF16), to_left(1))
        next_far = block(z ^ 2, cols)
        right = send((next_far + right.astype(F32)).astype(BF16), to_right(2))
        left = send((next_far + left.astype(F32)).astype(BF16), to_left(2))
        near = block(z ^ 1, cols)
        right = (jnp.where(z == 1, far, near) + right.astype(F32)).astype(BF16)
        left = (jnp.where(z == 2, far, near) + left.astype(F32)).astype(BF16)
        right, left = send(right, to_right(3)), send(left, to_left(3))
        return block(z, cols) + right.astype(F32) + left.astype(F32)

    sums = jnp.stack([summed(columns), summed(core_columns)])
    out = [
        lax.dynamic_slice(
            sums, (c ^ k, 0, (q ^ chip) * piece), (1, piece, piece)
        ).reshape(piece, piece)
        for c in range(2)
        for q in range(4)
    ]
    return jnp.concatenate(out, 1)


def solution(mesh):
    planes = tuple(mesh.shape[a] for a in AXES) == (4, 4, 2)
    return jax.shard_map(
        four_planes if planes else any_mesh,
        mesh=mesh,
        in_specs=(P(("pair", "col"), None), P("row", ("pair", "col")), P("pair"), P()),
        out_specs=P(("row", "pair"), "col"),
        check_vma=False,
    )
```

```python
import jax
import jax.numpy as jnp
from jax import lax
from jax.sharding import PartitionSpec as P

AXES = ("pair", "row", "col")
BF16 = jnp.bfloat16
F32 = jnp.float32


def rows_by_rows(a, b):
    return lax.dot_general(a, b, (((1,), (1,)), ((), ())), preferred_element_type=F32)


def columns_by_columns(a, b):
    return lax.dot_general(a, b, (((0,), (0,)), ((), ())), preferred_element_type=F32)


def scale_of(energies, frequency):
    return 2.0 * energies / (energies * energies + frequency[0] * frequency[0])


def any_mesh(integrals, inverse_factor, energies, frequency):
    n_col = lax.axis_size("col")
    q_cols = integrals.shape[1] // n_col
    local_rows = rows_by_rows(
        integrals, lax.all_gather(inverse_factor, ("pair", "col"), axis=1, tiled=True)
    )
    group_b = lax.all_gather(local_rows.astype(BF16), "col", axis=0, tiled=True)
    portion = lax.all_gather(group_b, "row", axis=1, tiled=True)
    col_b = lax.dynamic_slice_in_dim(
        portion, lax.axis_index("col") * q_cols, q_cols, axis=1
    )
    factor = scale_of(energies, frequency)
    scaled = (factor[:, None] * group_b.astype(F32)).astype(BF16)
    return lax.psum_scatter(
        columns_by_columns(scaled, col_b), "pair", scatter_dimension=0, tiled=True
    )


def route(target):
    def index(z, x, k, y):
        return ((z * 2 + x) * 2 + k) * 2 + y

    pairs = []
    for z in range(4):
        for x in range(2):
            for k in range(2):
                for y in range(2):
                    to = target(z, x, k, y)
                    if to is not None:
                        pairs.append((index(z, x, k, y), index(*to)))
    return pairs


def send(value, pairs):
    return lax.ppermute(value, AXES, pairs)


OVER_X = route(lambda z, x, k, y: (z, 1 - x, k, y))
OVER_Y = route(lambda z, x, k, y: (z, x, k, 1 - y))
OVER_XY = route(lambda z, x, k, y: (z, 1 - x, k, 1 - y))
OVER_CORE = route(lambda z, x, k, y: (z, x, 1 - k, y))


def along_z(step, allowed):
    def target(z, x, k, y):
        if 0 <= z + step < 4 and allowed(z, k):
            return (z + step, x, k, y)
        return None

    return route(target)


def row_block(stream, x, k):
    return 2 * (x if stream == 0 else 1 - x) + k


def z_hops(part, sign, step):
    def target(z, x, k, y):
        source, p = z - sign * (step - 1), part
        if 0 <= z + sign < 4 and 0 <= source < 4 and source <= 2 * p + k:
            return (z + sign, x, k, y)
        return None

    return route(target)


def four_planes(integrals, inverse_factor, energies, frequency):
    z = lax.axis_index("pair")
    row = lax.axis_index("row")
    x, k = row // 2, row % 2
    y = lax.axis_index("col")
    chip = 2 * x + y
    n_rows, width = inverse_factor.shape
    piece = n_rows // 4

    def ordered(flag, a, b, axis):
        return jnp.concatenate(
            [jnp.where(flag == 0, a, b), jnp.where(flag == 0, b, a)], axis
        )

    own, *others = lax.optimization_barrier(
        [
            lax.dynamic_slice_in_dim(inverse_factor, (chip ^ c) * piece, piece, 0)
            for c in range(4)
        ]
    )
    got = [send(q, r) for q, r in zip(others, (OVER_Y, OVER_X, OVER_XY))]
    same, other = ordered(y, own, got[0], 1), ordered(y, got[1], got[2], 1)
    parts = [jnp.where(x == 0, same, other), jnp.where(x == 0, other, same)]
    half = integrals.shape[0] // 2
    give = lax.dynamic_slice_in_dim(integrals, k * half, half, 0)
    from_y = send(give, OVER_Y)
    from_core = send(from_y, OVER_CORE)
    theirs = ordered(k, from_y, from_core, 0)

    def term(values, away):
        at = jnp.clip(z + away, 0, 3) * 2 * width
        return [
            rows_by_rows(lax.dynamic_slice_in_dim(a, at, 2 * width, 1), values)
            for a in (integrals, theirs)
        ]

    came = [[(parts[p], 0)] for p in range(2)]
    moving = [[parts[p], parts[p]] for p in range(2)]
    for step in (1, 2, 3):
        for d in (0, 1):
            for p in (0, 1):
                sign = 1 - 2 * d
                pairs = z_hops(p, sign, step)
                if pairs:
                    moving[p][d] = send(moving[p][d], pairs)
                    came[p].append((moving[p][d], -sign * step))
    totals = []
    for p in range(2):
        total = term(*came[p][0])
        for value, away in came[p][1:]:
            total = [t + m for t, m in zip(total, term(value, away))]
        totals.append(total)
    straight, across = [
        ordered(y, t[0].astype(BF16), t[1].astype(BF16), 0) for t in totals
    ]

    straight_y, across_y = send(straight, OVER_Y), send(across, OVER_Y)
    straight_x, across_x = send(straight, OVER_X), send(across, OVER_X)
    straight_xy, across_xy = send(straight_y, OVER_X), send(across_x, OVER_Y)
    lows = [straight, straight_y, straight_x, straight_xy]
    highs = [across, across_y, across_x, across_xy]
    rows = jnp.concatenate([jnp.where(x == 0, a, b) for a, b in zip(lows, highs)], 1)
    columns = jnp.concatenate(
        [jnp.where(y == 0, a, b) for a, b in zip(lows, highs)], 1
    )
    core_columns = send(columns, OVER_CORE)
    factor = scale_of(energies, frequency)
    scaled = (factor[:, None] * rows.astype(F32)).astype(BF16)

    def block(plane, cols):
        at = (plane ^ chip) * piece
        return columns_by_columns(lax.dynamic_slice_in_dim(scaled, at, piece, 1), cols)

    def to_right(hop):
        return along_z(1, lambda at, core: at < hop)

    def to_left(hop):
        return along_z(-1, lambda at, core: at > 3 - hop)

    def summed(cols):
        far = block(z ^ 3, cols)
        right = send(far.astype(BF16), to_right(1))
        left = send(far.astype(BF16), to_left(1))
        next_far = block(z ^ 2, cols)
        right = send((next_far + right.astype(F32)).astype(BF16), to_right(2))
        left = send((next_far + left.astype(F32)).astype(BF16), to_left(2))
        near = block(z ^ 1, cols)
        right = (jnp.where(z == 1, far, near) + right.astype(F32)).astype(BF16)
        left = (jnp.where(z == 2, far, near) + left.astype(F32)).astype(BF16)
        right, left = send(right, to_right(3)), send(left, to_left(3))
        return block(z, cols) + right.astype(F32) + left.astype(F32)

    out = []
    for part in (summed(columns), summed(core_columns)):
        a = [part[:, q * piece : (q + 1) * piece] for q in range(4)]
        a = [jnp.where(y == 0, a[q], a[q ^ 1]) for q in range(4)]
        out.append(jnp.concatenate([jnp.where(x == 0, a[q], a[q ^ 2]) for q in range(4)], 1))
    return ordered(k, *out, 1)


def solution(mesh):
    planes = tuple(mesh.shape[a] for a in AXES) == (4, 4, 2)
    return jax.shard_map(
        four_planes if planes else any_mesh,
        mesh=mesh,
        in_specs=(P(("pair", "col"), None), P("row", ("pair", "col")), P("pair"), P()),
        out_specs=P(("row", "pair"), "col"),
        check_vma=False,
    )
```

```python
import jax
import jax.numpy as jnp
from jax import lax
from jax.sharding import PartitionSpec as P

AXES = ("pair", "row", "col")
BF16 = jnp.bfloat16
F32 = jnp.float32


def rows_by_rows(a, b):
    return lax.dot_general(a, b, (((1,), (1,)), ((), ())), preferred_element_type=F32)


def columns_by_columns(a, b):
    return lax.dot_general(a, b, (((0,), (0,)), ((), ())), preferred_element_type=F32)


def scale_of(energies, frequency):
    return 2.0 * energies / (energies * energies + frequency[0] * frequency[0])


def any_mesh(integrals, inverse_factor, energies, frequency):
    n_col = lax.axis_size("col")
    q_cols = integrals.shape[1] // n_col
    local_rows = rows_by_rows(
        integrals, lax.all_gather(inverse_factor, ("pair", "col"), axis=1, tiled=True)
    )
    group_b = lax.all_gather(local_rows.astype(BF16), "col", axis=0, tiled=True)
    portion = lax.all_gather(group_b, "row", axis=1, tiled=True)
    col_b = lax.dynamic_slice_in_dim(
        portion, lax.axis_index("col") * q_cols, q_cols, axis=1
    )
    factor = scale_of(energies, frequency)
    scaled = (factor[:, None] * group_b.astype(F32)).astype(BF16)
    return lax.psum_scatter(
        columns_by_columns(scaled, col_b), "pair", scatter_dimension=0, tiled=True
    )


def route(target):
    def index(z, x, k, y):
        return ((z * 2 + x) * 2 + k) * 2 + y

    pairs = []
    for z in range(4):
        for x in range(2):
            for k in range(2):
                for y in range(2):
                    to = target(z, x, k, y)
                    if to is not None:
                        pairs.append((index(z, x, k, y), index(*to)))
    return pairs


def send(value, pairs):
    return lax.ppermute(value, AXES, pairs)


OVER_X = route(lambda z, x, k, y: (z, 1 - x, k, y))
OVER_Y = route(lambda z, x, k, y: (z, x, k, 1 - y))
OVER_XY = route(lambda z, x, k, y: (z, 1 - x, k, 1 - y))
OVER_CORE = route(lambda z, x, k, y: (z, x, 1 - k, y))


def along_z(step, allowed):
    def target(z, x, k, y):
        if 0 <= z + step < 4 and allowed(z, k):
            return (z + step, x, k, y)
        return None

    return route(target)


def row_block(stream, x, k):
    return 2 * (x if stream == 0 else 1 - x) + k


def z_hops(part, sign, step):
    def target(z, x, k, y):
        source, p = z - sign * (step - 1), part
        if 0 <= z + sign < 4 and 0 <= source < 4 and source <= 2 * p + k:
            return (z + sign, x, k, y)
        return None

    return route(target)


def after(value, *first):
    for array in first:
        value = value + 0 * array[:1, :1]
    return value


def four_planes(integrals, inverse_factor, energies, frequency):
    z = lax.axis_index("pair")
    row = lax.axis_index("row")
    x, k = row // 2, row % 2
    y = lax.axis_index("col")
    chip = 2 * x + y
    n_rows, width = inverse_factor.shape
    piece = n_rows // 4

    def ordered(flag, a, b, axis):
        return jnp.concatenate(
            [jnp.where(flag == 0, a, b), jnp.where(flag == 0, b, a)], axis
        )

    own, *others = lax.optimization_barrier(
        [
            lax.dynamic_slice_in_dim(inverse_factor, (chip ^ c) * piece, piece, 0)
            for c in range(4)
        ]
    )
    got = [send(q, r) for q, r in zip(others, (OVER_Y, OVER_X, OVER_XY))]
    same, other = ordered(y, own, got[0], 1), ordered(y, got[1], got[2], 1)
    parts = [jnp.where(x == 0, same, other), jnp.where(x == 0, other, same)]
    half = integrals.shape[0] // 2
    give = lax.dynamic_slice_in_dim(integrals, k * half, half, 0)
    from_y = send(give, OVER_Y)
    from_core = send(from_y, OVER_CORE)
    theirs = ordered(k, from_y, from_core, 0)

    def term(values, away):
        at = jnp.clip(z + away, 0, 3) * 2 * width
        return [
            rows_by_rows(lax.dynamic_slice_in_dim(a, at, 2 * width, 1), values)
            for a in (integrals, theirs)
        ]

    came = [[(parts[p], 0)] for p in range(2)]
    moving = [[parts[p], parts[p]] for p in range(2)]
    for step in (1, 2, 3):
        for d in (0, 1):
            for p in (0, 1):
                sign = 1 - 2 * d
                pairs = z_hops(p, sign, step)
                if pairs:
                    moving[p][d] = send(moving[p][d], pairs)
                    came[p].append((moving[p][d], -sign * step))
    totals = []
    for p in range(2):
        total = term(*came[p][0])
        for value, away in came[p][1:]:
            total = [t + m for t, m in zip(total, term(value, away))]
        totals.append(total)
    straight, across = [
        ordered(y, t[0].astype(BF16), t[1].astype(BF16), 0) for t in totals
    ]

    straight_y, straight_x = send(straight, OVER_Y), send(straight, OVER_X)
    across = after(across, straight_y, straight_x)
    across_y, across_x = send(across, OVER_Y), send(across, OVER_X)
    straight_xy, across_xy = send(straight_y, OVER_X), send(across_x, OVER_Y)
    lows = [straight, straight_y, straight_x, straight_xy]
    highs = [across, across_y, across_x, across_xy]
    rows = jnp.concatenate([jnp.where(x == 0, a, b) for a, b in zip(lows, highs)], 1)
    columns = jnp.concatenate(
        [jnp.where(y == 0, a, b) for a, b in zip(lows, highs)], 1
    )
    core_columns = send(columns, OVER_CORE)
    factor = scale_of(energies, frequency)
    scaled = (factor[:, None] * rows.astype(F32)).astype(BF16)

    def block(plane, cols):
        at = (plane ^ chip) * piece
        return columns_by_columns(lax.dynamic_slice_in_dim(scaled, at, piece, 1), cols)

    def to_right(hop):
        return along_z(1, lambda at, core: at < hop)

    def to_left(hop):
        return along_z(-1, lambda at, core: at > 3 - hop)

    def summed(cols):
        far = block(z ^ 3, cols)
        right = send(far.astype(BF16), to_right(1))
        left = send(far.astype(BF16), to_left(1))
        next_far = block(z ^ 2, cols)
        right = send((next_far + right.astype(F32)).astype(BF16), to_right(2))
        left = send((next_far + left.astype(F32)).astype(BF16), to_left(2))
        near = block(z ^ 1, cols)
        right = (jnp.where(z == 1, far, near) + right.astype(F32)).astype(BF16)
        left = (jnp.where(z == 2, far, near) + left.astype(F32)).astype(BF16)
        right, left = send(right, to_right(3)), send(left, to_left(3))
        return block(z, cols) + right.astype(F32) + left.astype(F32)

    out = []
    for part in (summed(columns), summed(core_columns)):
        a = [part[:, q * piece : (q + 1) * piece] for q in range(4)]
        a = [jnp.where(y == 0, a[q], a[q ^ 1]) for q in range(4)]
        out.append(jnp.concatenate([jnp.where(x == 0, a[q], a[q ^ 2]) for q in range(4)], 1))
    return ordered(k, *out, 1)


def solution(mesh):
    planes = tuple(mesh.shape[a] for a in AXES) == (4, 4, 2)
    return jax.shard_map(
        four_planes if planes else any_mesh,
        mesh=mesh,
        in_specs=(P(("pair", "col"), None), P("row", ("pair", "col")), P("pair"), P()),
        out_specs=P(("row", "pair"), "col"),
        check_vma=False,
    )
```

```python
import jax
import jax.numpy as jnp
from jax import lax
from jax.sharding import PartitionSpec as P

AXES = ("pair", "row", "col")
BF16 = jnp.bfloat16
F32 = jnp.float32


def rows_by_rows(a, b):
    return lax.dot_general(a, b, (((1,), (1,)), ((), ())), preferred_element_type=F32)


def columns_by_columns(a, b):
    return lax.dot_general(a, b, (((0,), (0,)), ((), ())), preferred_element_type=F32)


def scale_of(energies, frequency):
    return 2.0 * energies / (energies * energies + frequency[0] * frequency[0])


def any_mesh(integrals, inverse_factor, energies, frequency):
    n_col = lax.axis_size("col")
    q_cols = integrals.shape[1] // n_col
    local_rows = rows_by_rows(
        integrals, lax.all_gather(inverse_factor, ("pair", "col"), axis=1, tiled=True)
    )
    group_b = lax.all_gather(local_rows.astype(BF16), "col", axis=0, tiled=True)
    portion = lax.all_gather(group_b, "row", axis=1, tiled=True)
    col_b = lax.dynamic_slice_in_dim(
        portion, lax.axis_index("col") * q_cols, q_cols, axis=1
    )
    factor = scale_of(energies, frequency)
    scaled = (factor[:, None] * group_b.astype(F32)).astype(BF16)
    return lax.psum_scatter(
        columns_by_columns(scaled, col_b), "pair", scatter_dimension=0, tiled=True
    )


def route(target):
    def index(z, x, k, y):
        return ((z * 2 + x) * 2 + k) * 2 + y

    pairs = []
    for z in range(4):
        for x in range(2):
            for k in range(2):
                for y in range(2):
                    to = target(z, x, k, y)
                    if to is not None:
                        pairs.append((index(z, x, k, y), index(*to)))
    return pairs


def send(value, pairs):
    return lax.ppermute(value, AXES, pairs)


OVER_X = route(lambda z, x, k, y: (z, 1 - x, k, y))
OVER_Y = route(lambda z, x, k, y: (z, x, k, 1 - y))
OVER_XY = route(lambda z, x, k, y: (z, 1 - x, k, 1 - y))
OVER_CORE = route(lambda z, x, k, y: (z, x, 1 - k, y))


def along_z(step, allowed):
    def target(z, x, k, y):
        if 0 <= z + step < 4 and allowed(z, k):
            return (z + step, x, k, y)
        return None

    return route(target)


def row_block(stream, x, k):
    return 2 * (x if stream == 0 else 1 - x) + k


def z_hops(part, sign, step):
    def target(z, x, k, y):
        source, p = z - sign * (step - 1), part
        if 0 <= z + sign < 4 and 0 <= source < 4 and source <= 2 * p + k:
            return (z + sign, x, k, y)
        return None

    return route(target)


def after(value, *first):
    for array in first:
        value = value + 0 * array[:1]
    return value


def four_planes(integrals, inverse_factor, energies, frequency):
    z = lax.axis_index("pair")
    row = lax.axis_index("row")
    x, k = row // 2, row % 2
    y = lax.axis_index("col")
    chip = 2 * x + y
    n_rows, width = inverse_factor.shape
    piece = n_rows // 4

    def ordered(flag, a, b, axis):
        return jnp.concatenate(
            [jnp.where(flag == 0, a, b), jnp.where(flag == 0, b, a)], axis
        )

    own, *others = lax.optimization_barrier(
        [
            lax.dynamic_slice_in_dim(inverse_factor, (chip ^ c) * piece, piece, 0)
            for c in range(4)
        ]
    )
    got = [send(q, r) for q, r in zip(others, (OVER_Y, OVER_X, OVER_XY))]
    same, other = ordered(y, own, got[0], 1), ordered(y, got[1], got[2], 1)
    parts = [jnp.where(x == 0, same, other), jnp.where(x == 0, other, same)]
    half = integrals.shape[0] // 2
    give = lax.dynamic_slice_in_dim(integrals, k * half, half, 0)
    from_y = send(give, OVER_Y)
    from_core = send(from_y, OVER_CORE)
    theirs = ordered(k, from_y, from_core, 0)

    def term(values, away):
        at = jnp.clip(z + away, 0, 3) * 2 * width
        return [
            rows_by_rows(lax.dynamic_slice_in_dim(a, at, 2 * width, 1), values)
            for a in (integrals, theirs)
        ]

    came = [[(parts[p], 0)] for p in range(2)]
    moving = [[parts[p], parts[p]] for p in range(2)]
    for step in (1, 2, 3):
        for d in (0, 1):
            for p in (0, 1):
                sign = 1 - 2 * d
                pairs = z_hops(p, sign, step)
                if pairs:
                    moving[p][d] = send(moving[p][d], pairs)
                    came[p].append((moving[p][d], -sign * step))
    totals = []
    for p in range(2):
        total = term(*came[p][0])
        for value, away in came[p][1:]:
            total = [t + m for t, m in zip(total, term(value, away))]
        totals.append(total)
    straight, across = [
        ordered(y, t[0].astype(BF16), t[1].astype(BF16), 0) for t in totals
    ]

    straight_y, straight_x = send(straight, OVER_Y), send(straight, OVER_X)
    across = after(across, straight_x)
    across_y, across_x = send(across, OVER_Y), send(across, OVER_X)
    straight_xy, across_xy = send(straight_y, OVER_X), send(across_x, OVER_Y)
    lows = [straight, straight_y, straight_x, straight_xy]
    highs = [across, across_y, across_x, across_xy]
    rows = jnp.concatenate([jnp.where(x == 0, a, b) for a, b in zip(lows, highs)], 1)
    columns = jnp.concatenate(
        [jnp.where(y == 0, a, b) for a, b in zip(lows, highs)], 1
    )
    core_columns = send(columns, OVER_CORE)
    factor = scale_of(energies, frequency)
    scaled = (factor[:, None] * rows.astype(F32)).astype(BF16)

    def block(plane, cols):
        at = (plane ^ chip) * piece
        return columns_by_columns(lax.dynamic_slice_in_dim(scaled, at, piece, 1), cols)

    def to_right(hop):
        return along_z(1, lambda at, core: at < hop)

    def to_left(hop):
        return along_z(-1, lambda at, core: at > 3 - hop)

    def summed(cols):
        far = block(z ^ 3, cols)
        right = send(far.astype(BF16), to_right(1))
        left = send(far.astype(BF16), to_left(1))
        next_far = block(z ^ 2, cols)
        right = send((next_far + right.astype(F32)).astype(BF16), to_right(2))
        left = send((next_far + left.astype(F32)).astype(BF16), to_left(2))
        near = block(z ^ 1, cols)
        right = (jnp.where(z == 1, far, near) + right.astype(F32)).astype(BF16)
        left = (jnp.where(z == 2, far, near) + left.astype(F32)).astype(BF16)
        right, left = send(right, to_right(3)), send(left, to_left(3))
        return block(z, cols) + right.astype(F32) + left.astype(F32)

    out = []
    for part in (summed(columns), summed(core_columns)):
        a = [part[:, q * piece : (q + 1) * piece] for q in range(4)]
        a = [jnp.where(y == 0, a[q], a[q ^ 1]) for q in range(4)]
        out.append(jnp.concatenate([jnp.where(x == 0, a[q], a[q ^ 2]) for q in range(4)], 1))
    return ordered(k, *out, 1)


def solution(mesh):
    planes = tuple(mesh.shape[a] for a in AXES) == (4, 4, 2)
    return jax.shard_map(
        four_planes if planes else any_mesh,
        mesh=mesh,
        in_specs=(P(("pair", "col"), None), P("row", ("pair", "col")), P("pair"), P()),
        out_specs=P(("row", "pair"), "col"),
        check_vma=False,
    )
```

```python
import jax
import jax.numpy as jnp
from jax import lax
from jax.sharding import PartitionSpec as P

AXES = ("pair", "row", "col")
BF16 = jnp.bfloat16
F32 = jnp.float32


def rows_by_rows(a, b):
    return lax.dot_general(a, b, (((1,), (1,)), ((), ())), preferred_element_type=F32)


def columns_by_columns(a, b):
    return lax.dot_general(a, b, (((0,), (0,)), ((), ())), preferred_element_type=F32)


def scale_of(energies, frequency):
    return 2.0 * energies / (energies * energies + frequency[0] * frequency[0])


def any_mesh(integrals, inverse_factor, energies, frequency):
    n_col = lax.axis_size("col")
    q_cols = integrals.shape[1] // n_col
    local_rows = rows_by_rows(
        integrals, lax.all_gather(inverse_factor, ("pair", "col"), axis=1, tiled=True)
    )
    group_b = lax.all_gather(local_rows.astype(BF16), "col", axis=0, tiled=True)
    portion = lax.all_gather(group_b, "row", axis=1, tiled=True)
    col_b = lax.dynamic_slice_in_dim(
        portion, lax.axis_index("col") * q_cols, q_cols, axis=1
    )
    factor = scale_of(energies, frequency)
    scaled = (factor[:, None] * group_b.astype(F32)).astype(BF16)
    return lax.psum_scatter(
        columns_by_columns(scaled, col_b), "pair", scatter_dimension=0, tiled=True
    )


def route(target):
    def index(z, x, k, y):
        return ((z * 2 + x) * 2 + k) * 2 + y

    pairs = []
    for z in range(4):
        for x in range(2):
            for k in range(2):
                for y in range(2):
                    to = target(z, x, k, y)
                    if to is not None:
                        pairs.append((index(z, x, k, y), index(*to)))
    return pairs


def send(value, pairs):
    return lax.ppermute(value, AXES, pairs)


OVER_X = route(lambda z, x, k, y: (z, 1 - x, k, y))
OVER_Y = route(lambda z, x, k, y: (z, x, k, 1 - y))
OVER_XY = route(lambda z, x, k, y: (z, 1 - x, k, 1 - y))
OVER_CORE = route(lambda z, x, k, y: (z, x, 1 - k, y))


def along_z(step, allowed):
    def target(z, x, k, y):
        if 0 <= z + step < 4 and allowed(z, k):
            return (z + step, x, k, y)
        return None

    return route(target)


def row_block(stream, x, k):
    return 2 * (x if stream == 0 else 1 - x) + k


def z_hops(part, sign, step):
    def target(z, x, k, y):
        source, p = z - sign * (step - 1), part
        if 0 <= z + sign < 4 and 0 <= source < 4 and source <= 2 * p + k:
            return (z + sign, x, k, y)
        return None

    return route(target)


def after(value, *first):
    for array in first:
        value = value + 0 * array[:1]
    return value


def four_planes(integrals, inverse_factor, energies, frequency):
    z = lax.axis_index("pair")
    row = lax.axis_index("row")
    x, k = row // 2, row % 2
    y = lax.axis_index("col")
    chip = 2 * x + y
    n_rows, width = inverse_factor.shape
    piece = n_rows // 4

    def ordered(flag, a, b, axis):
        return jnp.concatenate(
            [jnp.where(flag == 0, a, b), jnp.where(flag == 0, b, a)], axis
        )

    own, *others = lax.optimization_barrier(
        [
            lax.dynamic_slice_in_dim(inverse_factor, (chip ^ c) * piece, piece, 0)
            for c in range(4)
        ]
    )
    got = [send(q, r) for q, r in zip(others, (OVER_Y, OVER_X, OVER_XY))]
    same, other = ordered(y, own, got[0], 1), ordered(y, got[1], got[2], 1)
    parts = [jnp.where(x == 0, same, other), jnp.where(x == 0, other, same)]
    half = integrals.shape[0] // 2
    give = lax.dynamic_slice_in_dim(integrals, k * half, half, 0)
    from_y = send(give, OVER_Y)
    from_core = send(from_y, OVER_CORE)
    theirs = ordered(k, from_y, from_core, 0)

    def term(values, away):
        at = jnp.clip(z + away, 0, 3) * 2 * width
        return [
            rows_by_rows(lax.dynamic_slice_in_dim(a, at, 2 * width, 1), values)
            for a in (integrals, theirs)
        ]

    came = [[(parts[p], 0)] for p in range(2)]
    moving = [[parts[p], parts[p]] for p in range(2)]
    for step in (1, 2, 3):
        for d in (0, 1):
            for p in (0, 1):
                sign = 1 - 2 * d
                pairs = z_hops(p, sign, step)
                if pairs:
                    moving[p][d] = send(moving[p][d], pairs)
                    came[p].append((moving[p][d], -sign * step))
    totals = []
    for p in range(2):
        total = term(*came[p][0])
        for value, away in came[p][1:]:
            total = [t + m for t, m in zip(total, term(value, away))]
        totals.append(total)
    straight, across = [
        ordered(y, t[0].astype(BF16), t[1].astype(BF16), 0) for t in totals
    ]

    straight_y, straight_x = send(straight, OVER_Y), send(straight, OVER_X)
    across = after(across, straight_x)
    across_y, across_x = send(across, OVER_Y), send(across, OVER_X)
    straight_xy, across_xy = send(straight_y, OVER_X), send(across_x, OVER_Y)
    lows = [straight, straight_y, straight_x, straight_xy]
    highs = [across, across_y, across_x, across_xy]
    rows = jnp.concatenate([jnp.where(x == 0, a, b) for a, b in zip(lows, highs)], 1)
    columns = jnp.concatenate(
        [jnp.where(y == 0, a, b) for a, b in zip(lows, highs)], 1
    )
    core_columns = send(columns, OVER_CORE)
    factor = scale_of(energies, frequency)
    scaled = (factor[:, None] * rows.astype(F32)).astype(BF16)

    def block(plane, cols):
        at = (plane ^ chip) * piece
        return columns_by_columns(lax.dynamic_slice_in_dim(scaled, at, piece, 1), cols)

    def to_right(hop):
        return along_z(1, lambda at, core: at < hop)

    def to_left(hop):
        return along_z(-1, lambda at, core: at > 3 - hop)

    def summed(cols):
        far = block(z ^ 3, cols)
        ends = send(far.astype(BF16), to_right(1) + to_left(1))
        message = (block(z ^ 2, cols) + ends.astype(F32)).astype(BF16)
        right, left = send(message, to_right(2)), send(message, to_left(2))
        near = block(z ^ 1, cols)
        right = (jnp.where(z == 1, far, near) + right.astype(F32)).astype(BF16)
        left = (jnp.where(z == 2, far, near) + left.astype(F32)).astype(BF16)
        right, left = send(right, to_right(3)), send(left, to_left(3))
        return block(z, cols) + right.astype(F32) + left.astype(F32)

    out = []
    for part in (summed(columns), summed(core_columns)):
        a = [part[:, q * piece : (q + 1) * piece] for q in range(4)]
        a = [jnp.where(y == 0, a[q], a[q ^ 1]) for q in range(4)]
        out.append(jnp.concatenate([jnp.where(x == 0, a[q], a[q ^ 2]) for q in range(4)], 1))
    return ordered(k, *out, 1)


def solution(mesh):
    planes = tuple(mesh.shape[a] for a in AXES) == (4, 4, 2)
    return jax.shard_map(
        four_planes if planes else any_mesh,
        mesh=mesh,
        in_specs=(P(("pair", "col"), None), P("row", ("pair", "col")), P("pair"), P()),
        out_specs=P(("row", "pair"), "col"),
        check_vma=False,
    )
```
